128 devices in a mesh: gx: 8 (over z_lo, x), gy: 16 (over z_hi, y, core).
Axes of the slice: x: 4, y: 4, z: 4 (z_hi: 2, z_lo: 2; z = z_hi * 2 + z_lo), core: 2. Of those that a mesh axis runs over, the one named last changes fastest.
Arguments:
- source: float32 [2, 1024, 64, 512], P(None, ('gx', 'gy')), may hold values from -6 to 6
- weights: float32 [7, 2, 1024, 64, 128], P(None, None, ('gx', 'gy')), may hold values from -0.375 to 0.375
- interp: float32 [2, 1024, 64, 128], P(None, ('gx', 'gy')), may hold values from -0.5 to 0.5
Outputs:
- far_field: float32 [2, 512, 1024, 128], P(None, ('gx', 'gy'))
The draws below stay inside these ranges and needn't reach their ends.
All inputs are finite; a program needn't handle non-finite values.
Results may differ from the reference program's by a relative error of at most 0.0001.
Values sent between devices are 32-bit elements; how exact they have to be, the bound alone decides.
No kernel may reach another device: no remote copies, remote signals or barrier semaphores. Data moves between devices by JAX's collectives and lax.ppermute only.
A program may use at most 64 MiB of HBM per device.

```python
import jax
import jax.numpy as jnp
from jax import lax

R = 64
Q = 128
K = 8
S = 512
P_SIZE = 1024
LV = 7


def block_scale(stream_key, extent, cuts, least, top_value):
    def one(axis_at, shards_of):
        steps = jax.random.uniform(jax.random.fold_in(jax.random.fold_in(stream_key, 6), axis_at), (shards_of,), jnp.float32, least / len(cuts), top_value / len(cuts))
        return jnp.repeat(jnp.exp(steps), extent[axis_at] // shards_of).reshape((-1,) + (1,) * (len(extent) - axis_at - 1))

    factor_of = one(*cuts[0])
    for cut in cuts[1:]:
        factor_of = factor_of * one(*cut)
    return factor_of


def scatter_about(key, shape, scale, bound, cuts=(), held_as=jnp.bfloat16):
    loudness = block_scale(key, shape, cuts, -0.22, 0.18) if cuts else 1.0
    array = jax.random.normal(key, shape, jnp.float32) * scale * loudness
    return jnp.minimum(jnp.maximum(array, -bound), bound).astype(held_as)


def setup_inputs(seed: int = 0) -> dict:
    key_of = jax.random.split(jax.random.key(seed), 4)
    return {
        "source": scatter_about(key_of[0], (2, P_SIZE, R, S), 1.0, 6.0, ((1, 128),), jnp.float32),
        "weights": scatter_about(key_of[1], (LV, 2, P_SIZE, R, 2 * R), (4 * R) ** -0.5, 0.375, ((2, 128),), jnp.float32),
        "interp": scatter_about(key_of[2], (2, P_SIZE, R, Q), (2 * R) ** -0.5, 0.5, ((1, 128),), jnp.float32),
    }


def mix(w_part, c_part):
    return jnp.einsum('gbmrj,gmjs->gbmrs', w_part, c_part, precision=lax.Precision.HIGHEST)


def reference(source, weights, interp):
    state = source
    for level in range(LV):
        span = K * 2 ** level
        groups = P_SIZE // (2 * span)
        split = state.reshape(2, groups, 2, span, R, S)
        stacked = jnp.concatenate([split[:, :, 0], split[:, :, 1]], axis=3)
        blocks = weights[level].reshape(2, groups, 2, span, R, 2 * R)
        real = mix(blocks[0], stacked[0]) - mix(blocks[1], stacked[1])
        imag = mix(blocks[0], stacked[1]) + mix(blocks[1], stacked[0])
        state = jnp.stack([real, imag]).reshape(2, P_SIZE, R, S)

    def proj(a, b):
        return jnp.einsum('prq,prs->spq', a, b, precision=lax.Precision.HIGHEST)

    real = proj(interp[0], state[0]) - proj(interp[1], state[1])
    imag = proj(interp[0], state[1]) + proj(interp[1], state[0])
    return jnp.stack([real, imag])
```

```python
import jax
import jax.numpy as jnp
from jax import lax
from jax.experimental import pallas as pl
from jax.experimental.pallas import tpu as pltpu
from jax.sharding import PartitionSpec as P

AXES = ("gx", "gy")
TILE = 256
VMEM_BYTES = 48 * 1024 * 1024


def halves(value):
    high = value.astype(jnp.bfloat16)
    return high, (value - high.astype(jnp.float32)).astype(jnp.bfloat16)


def dot3(a_high, a_low, b_high, b_low):
    rows = a_high.shape[0]
    both = jnp.dot(jnp.concatenate([a_high, a_low], 0), b_high, preferred_element_type=jnp.float32)
    return both[:rows] + both[rows:] + jnp.dot(a_high, b_low, preferred_element_type=jnp.float32)


def real_rows(real, imag):
    return jnp.concatenate([jnp.concatenate([real, -imag], 1), jnp.concatenate([imag, real], 1)], 0)


def first_level_kernel(bit_ref, own_ref, other_ref, w_ref, out_ref):
    swap = bit_ref[0] == 1
    real, imag = w_ref[0, 0, 0], w_ref[0, 1, 0]
    real = jnp.where(swap, pltpu.roll(real, 64, 1), real)
    imag = jnp.where(swap, pltpu.roll(imag, 64, 1), imag)
    block = real_rows(real, imag)
    coeffs = jnp.concatenate([own_ref[0, 0], other_ref[0, 0], own_ref[1, 0], other_ref[1, 0]], 0)
    out_ref[0] = dot3(*halves(block), *halves(coeffs))


def first_level(bit, own, other, weights):
    _, boxes, rank, frames = own.shape
    state = pl.BlockSpec((2, 1, rank, frames), lambda k, bit: (0, k, 0, 0))
    return pl.pallas_call(
        first_level_kernel,
        out_shape=jax.ShapeDtypeStruct((boxes, 2 * rank, frames), jnp.float32),
        grid_spec=pltpu.PrefetchScalarGridSpec(
            num_scalar_prefetch=1,
            grid=(boxes,),
            in_specs=[
                state,
                state,
                pl.BlockSpec((1, 2, 1, rank, 2 * rank), lambda k, bit: (0, 0, k, 0, 0)),
            ],
            out_specs=pl.BlockSpec((1, 2 * rank, frames), lambda k, bit: (k, 0, 0)),
        ),
        compiler_params=pltpu.CompilerParams(vmem_limit_bytes=VMEM_BYTES),
        cost_estimate=pl.CostEstimate(flops=900_000_000, bytes_accessed=7_000_000, transcendentals=0),
        name="first_level",
    )(bit, own, other, weights)


def one_level(state_ref, w_ref, at, mask):
    boxes = state_ref.shape[0]
    rank = state_ref.shape[1] // 2
    for low in range(boxes):
        if low & mask:
            continue
        high = low | mask
        block = jnp.concatenate(
            [real_rows(w_ref[low, at, 0], w_ref[low, at, 1]), real_rows(w_ref[high, at, 0], w_ref[high, at, 1])], 0
        )
        coeffs = jnp.concatenate(
            [state_ref[low, :rank], state_ref[high, :rank], state_ref[low, rank:], state_ref[high, rank:]], 0
        )
        new = dot3(*halves(block), *halves(coeffs))
        state_ref[low] = new[: 2 * rank]
        state_ref[high] = new[2 * rank :]


def three_levels_kernel(in_ref, w_ref, out_ref):
    out_ref[...] = in_ref[...]
    for at in range(3):
        one_level(out_ref, w_ref, at, 1 << at)


def three_levels(state, weights):
    boxes, rows, frames = state.shape
    tile = pl.BlockSpec((boxes, rows, TILE), lambda i: (0, 0, i))
    return pl.pallas_call(
        three_levels_kernel,
        out_shape=jax.ShapeDtypeStruct(state.shape, jnp.float32),
        grid=(frames // TILE,),
        in_specs=[tile, pl.BlockSpec((boxes, 3, 2, rows // 2, rows), lambda i: (0, 0, 0, 0, 0))],
        out_specs=tile,
        compiler_params=pltpu.CompilerParams(vmem_limit_bytes=VMEM_BYTES),
        cost_estimate=pl.CostEstimate(flops=2_700_000_000, bytes_accessed=6_000_000, transcendentals=0),
        name="three_levels",
    )(state, weights)


def last_levels_kernel(in_ref, w_ref, out_ref, state_ref):
    state_ref[...] = in_ref[...]
    for at in range(3):
        one_level(state_ref, w_ref, at, 1 << at)
    boxes = state_ref.shape[0]
    for box in range(boxes):
        real, imag = w_ref[box, 3, 0], w_ref[box, 3, 1]
        block = jnp.concatenate([jnp.concatenate([real, imag], 1), jnp.concatenate([-imag, real], 1)], 0)
        samples = dot3(*halves(jnp.transpose(state_ref[box])), *halves(block))
        columns = real.shape[1]
        count = samples.shape[0]
        out_ref[pl.ds(box, count, stride=2 * boxes), :] = samples[:, :columns]
        out_ref[pl.ds(boxes + box, count, stride=2 * boxes), :] = samples[:, columns:]


def last_levels(state, weights):
    boxes, rows, frames = state.shape
    return pl.pallas_call(
        last_levels_kernel,
        out_shape=jax.ShapeDtypeStruct((frames * 2 * boxes, rows), jnp.float32),
        grid=(frames // TILE,),
        in_specs=[
            pl.BlockSpec((boxes, rows, TILE), lambda i: (0, 0, i)),
            pl.BlockSpec((boxes, 4, 2, rows // 2, rows), lambda i: (0, 0, 0, 0, 0)),
        ],
        out_specs=pl.BlockSpec((TILE * 2 * boxes, rows), lambda i: (i, 0)),
        scratch_shapes=[pltpu.VMEM((boxes, rows, TILE), jnp.float32)],
        compiler_params=pltpu.CompilerParams(vmem_limit_bytes=VMEM_BYTES),
        cost_estimate=pl.CostEstimate(flops=3_600_000_000, bytes_accessed=8_000_000, transcendentals=0),
        name="last_levels",
    )(state, weights)


def on_device(source, weights, interp):
    groups_y = [[g * 16 + h * 2 + c for h in range(8)] for g in range(8) for c in range(2)]

    def swap_y(value):
        return lax.all_to_all(value, AXES, 0, 0, axis_index_groups=groups_y, tiled=True)

    def swap_x(value):
        return lax.all_to_all(value, "gx", 0, 0, tiled=True)

    bit = (lax.axis_index("gy") & 1).astype(jnp.int32).reshape(1)
    other = lax.ppermute(source, "gy", [(i, i ^ 1) for i in range(16)])
    moved = jnp.concatenate([weights[1:], interp[None]], 0).transpose(2, 0, 1, 3, 4)
    moved = swap_y(moved)
    late = swap_x(moved[:, 3:])
    state = first_level(bit, source, other, weights)
    state = swap_y(state)
    state = three_levels(state, moved)
    state = swap_x(state)
    samples = last_levels(state, late)
    samples = samples.reshape(128, -1, samples.shape[-1])
    samples = lax.all_to_all(samples, AXES, 0, 0, tiled=True)
    samples = samples.reshape(8, 8, 2, 4, 2, 8, 128).transpose(4, 3, 5, 0, 2, 1, 6)
    return samples.reshape(2, 4, 1024, 128)


def solution(mesh):
    return jax.shard_map(
        on_device,
        mesh=mesh,
        in_specs=(
            P(None, ("gx", "gy"), None, None),
            P(None, None, ("gx", "gy"), None, None),
            P(None, ("gx", "gy"), None, None),
        ),
        out_specs=P(None, ("gx", "gy"), None, None),
        check_vma=False,
    )
```

```python
import jax
import jax.numpy as jnp
from jax import lax
from jax.experimental import pallas as pl
from jax.experimental.pallas import tpu as pltpu
from jax.sharding import PartitionSpec as P

AXES = ("gx", "gy")
TILE = 256
VMEM_BYTES = 48 * 1024 * 1024
ALL_VMEM_BYTES = 60 * 1024 * 1024


def halves(value):
    high = value.astype(jnp.bfloat16)
    return high, (value - high.astype(jnp.float32)).astype(jnp.bfloat16)


def dot3(a_high, a_low, b_high, b_low):
    rows = a_high.shape[0]
    both = jnp.dot(jnp.concatenate([a_high, a_low], 0), b_high, preferred_element_type=jnp.float32)
    return both[:rows] + both[rows:] + jnp.dot(a_high, b_low, preferred_element_type=jnp.float32)


def real_rows(real, imag):
    return jnp.concatenate([jnp.concatenate([real, -imag], 1), jnp.concatenate([imag, real], 1)], 0)


def first_level_kernel(bit_ref, own_ref, other_ref, w_ref, out_ref):
    swap = bit_ref[0] == 1
    real, imag = w_ref[0, 0, 0], w_ref[0, 1, 0]
    real = jnp.where(swap, pltpu.roll(real, 64, 1), real)
    imag = jnp.where(swap, pltpu.roll(imag, 64, 1), imag)
    block = real_rows(real, imag)
    coeffs = jnp.concatenate([own_ref[0, 0], other_ref[0, 0], own_ref[1, 0], other_ref[1, 0]], 0)
    out_ref[0] = dot3(*halves(block), *halves(coeffs))


def first_level(bit, own, other, weights):
    _, boxes, rank, frames = own.shape
    state = pl.BlockSpec((2, 1, rank, frames), lambda k, bit: (0, k, 0, 0))
    return pl.pallas_call(
        first_level_kernel,
        out_shape=jax.ShapeDtypeStruct((boxes, 2 * rank, frames), jnp.float32),
        grid_spec=pltpu.PrefetchScalarGridSpec(
            num_scalar_prefetch=1,
            grid=(boxes,),
            in_specs=[
                state,
                state,
                pl.BlockSpec((1, 2, 1, rank, 2 * rank), lambda k, bit: (0, 0, k, 0, 0)),
            ],
            out_specs=pl.BlockSpec((1, 2 * rank, frames), lambda k, bit: ((k & 3) * 2 + (k >> 2), 0, 0)),
        ),
        compiler_params=pltpu.CompilerParams(vmem_limit_bytes=VMEM_BYTES),
        cost_estimate=pl.CostEstimate(flops=900_000_000, bytes_accessed=7_000_000, transcendentals=0),
        name="first_level",
    )(bit, own, other, weights)


def one_level(state_ref, w_ref, at, pairs):
    rank = state_ref.shape[1] // 2
    for (low, w_low), (high, w_high) in pairs:
        block = jnp.concatenate(
            [real_rows(w_ref[w_low, at, 0], w_ref[w_low, at, 1]), real_rows(w_ref[w_high, at, 0], w_ref[w_high, at, 1])], 0
        )
        coeffs = jnp.concatenate(
            [state_ref[low, :rank], state_ref[high, :rank], state_ref[low, rank:], state_ref[high, rank:]], 0
        )
        new = dot3(*halves(block), *halves(coeffs))
        state_ref[low] = new[: 2 * rank]
        state_ref[high] = new[2 * rank :]


def pairs_of(mask):
    return [((b, b), (b | mask, b | mask)) for b in range(8) if not b & mask]


def y_levels_kernel(in_ref, w_ref, out_ref):
    out_ref[...] = in_ref[...]
    for at, mask in enumerate((2, 4)):
        one_level(out_ref, w_ref, at, pairs_of(mask))


def y_levels(state, weights):
    boxes, rows, frames = state.shape
    tile = pl.BlockSpec((boxes, rows, TILE), lambda i: (0, 0, i))
    return pl.pallas_call(
        y_levels_kernel,
        out_shape=jax.ShapeDtypeStruct(state.shape, jnp.float32),
        grid=(frames // TILE,),
        in_specs=[tile, pl.BlockSpec(weights.shape, lambda i: (0, 0, 0, 0, 0))],
        out_specs=tile,
        compiler_params=pltpu.CompilerParams(vmem_limit_bytes=ALL_VMEM_BYTES),
        cost_estimate=pl.CostEstimate(flops=1_800_000_000, bytes_accessed=5_000_000, transcendentals=0),
        name="y_levels",
    )(state, weights)


def z_level_kernel(me_ref, in_ref, keep_ref, came_ref, out_ref, w_ref):
    w_ref[me_ref[1], 0] = keep_ref[0]
    w_ref[1 - me_ref[1], 0] = came_ref[0]
    out_ref[...] = in_ref[...]
    one_level(out_ref, w_ref, 0, [((0, 0), (1, 1))])


def z_level(me, state, keep, came):
    boxes, rows, frames = state.shape
    pair = pl.BlockSpec((2, rows, frames), lambda i, me: (i, 0, 0))
    block = pl.BlockSpec((1,) + keep.shape[1:], lambda i, me: (i, 0, 0, 0))
    return pl.pallas_call(
        z_level_kernel,
        out_shape=jax.ShapeDtypeStruct(state.shape, jnp.float32),
        grid_spec=pltpu.PrefetchScalarGridSpec(
            num_scalar_prefetch=1,
            grid=(boxes // 2,),
            in_specs=[pair, block, block],
            out_specs=pair,
            scratch_shapes=[pltpu.VMEM((2, 1) + keep.shape[1:], jnp.float32)],
        ),
        compiler_params=pltpu.CompilerParams(vmem_limit_bytes=VMEM_BYTES),
        cost_estimate=pl.CostEstimate(flops=900_000_000, bytes_accessed=4_500_000, transcendentals=0),
        name="z_level",
    )(me, state, keep, came)


def last_levels_kernel(me_ref, in_ref, *refs):
    *late_refs, out_ref, w_ref, state_ref = refs

    @pl.when(pl.program_id(0) == 0)
    def _():
        for i, late_ref in enumerate(late_refs):
            for j in range(2):
                w_ref[(me_ref[0] ^ i) * 2 + (me_ref[1] ^ j)] = late_ref[j]

    state_ref[...] = in_ref[...]
    for at, mask in enumerate((2, 4, 1)):
        one_level(state_ref, w_ref, at, pairs_of(mask))
    boxes = state_ref.shape[0]
    for box in range(boxes):
        real, imag = w_ref[box, 3, 0], w_ref[box, 3, 1]
        block = jnp.concatenate([jnp.concatenate([real, imag], 1), jnp.concatenate([-imag, real], 1)], 0)
        samples = dot3(*halves(jnp.transpose(state_ref[box])), *halves(block))
        columns = real.shape[1]
        count = samples.shape[0]
        out_ref[pl.ds(box, count, stride=2 * boxes), :] = samples[:, :columns]
        out_ref[pl.ds(boxes + box, count, stride=2 * boxes), :] = samples[:, columns:]


def last_levels(me, state, late):
    boxes, rows, frames = state.shape
    return pl.pallas_call(
        last_levels_kernel,
        out_shape=jax.ShapeDtypeStruct((frames * 2 * boxes, rows), jnp.float32),
        grid_spec=pltpu.PrefetchScalarGridSpec(
            num_scalar_prefetch=1,
            grid=(frames // TILE,),
            in_specs=[pl.BlockSpec((boxes, rows, TILE), lambda i, me: (0, 0, i))]
            + [pl.BlockSpec(late[0].shape, lambda i, me: (0, 0, 0, 0, 0))] * 4,
            out_specs=pl.BlockSpec((TILE * 2 * boxes, rows), lambda i, me: (i, 0)),
            scratch_shapes=[
                pltpu.VMEM((boxes,) + late[0].shape[1:], jnp.float32),
                pltpu.VMEM((boxes, rows, TILE), jnp.float32),
            ],
        ),
        compiler_params=pltpu.CompilerParams(vmem_limit_bytes=VMEM_BYTES),
        cost_estimate=pl.CostEstimate(flops=3_600_000_000, bytes_accessed=8_000_000, transcendentals=0),
        name="last_levels",
    )(me, state, *late)


def early_kernel(w_ref, out_ref):
    for box in range(8):
        for part in range(2):
            out_ref[(box & 3) * 2 + (box >> 2), 0, part] = w_ref[0, part, box]


def early_blocks(weights):
    _, _, boxes, rank, columns = weights.shape
    return pl.pallas_call(
        early_kernel,
        out_shape=jax.ShapeDtypeStruct((boxes, 2, 2, rank, columns), jnp.float32),
        grid=(2,),
        in_specs=[pl.BlockSpec((1, 2, boxes, rank, columns), lambda i: (i + 1, 0, 0, 0, 0))],
        out_specs=pl.BlockSpec((boxes, 1, 2, rank, columns), lambda i: (0, i, 0, 0, 0)),
        compiler_params=pltpu.CompilerParams(vmem_limit_bytes=ALL_VMEM_BYTES),
        cost_estimate=pl.CostEstimate(flops=0, bytes_accessed=2_000_000, transcendentals=0),
        name="early_blocks",
    )(weights)


def late_kernel(me_ref, w_ref, interp_ref, keep1_ref, keep2_ref, give1_ref, give2_ref, keep3_ref, give3_ref):
    step = pl.program_id(0)
    last = pl.num_programs(0) - 1
    x, z_hi = me_ref[0], me_ref[1]

    @pl.when(step == 0)
    def _():
        for low in range(4):
            for part in range(2):
                keep3_ref[low, part] = w_ref[0, part, low + 4 * z_hi]
                give3_ref[low, part] = w_ref[0, part, low + 4 * (1 - z_hi)]

    def put(block):
        for at, keep_ref, give_ref in ((0, keep1_ref, give1_ref), (2, keep2_ref, give2_ref)):
            for i in range(2):
                for part in range(2):
                    keep_ref[i, 0, part] = block(part, (x ^ (at + i)) + 4 * z_hi)
                    give_ref[i, 0, part] = block(part, (x ^ (at + i)) + 4 * (1 - z_hi))

    @pl.when((step > 0) & (step < last))
    def _():
        put(lambda part, box: w_ref[0, part, box])

    @pl.when(step == last)
    def _():
        put(lambda part, box: interp_ref[part, box])


def late_blocks(me, weights, interp):
    levels, _, boxes, rank, columns = weights.shape
    half = jax.ShapeDtypeStruct((2, 4, 2, rank, columns), jnp.float32)
    third = jax.ShapeDtypeStruct((4, 2, rank, columns), jnp.float32)
    half_spec = pl.BlockSpec((2, 1, 2, rank, columns), lambda i, me: (0, jnp.maximum(i - 1, 0), 0, 0, 0))
    third_spec = pl.BlockSpec((4, 2, rank, columns), lambda i, me: (0, 0, 0, 0))
    return pl.pallas_call(
        late_kernel,
        out_shape=[half, half, half, half, third, third],
        grid_spec=pltpu.PrefetchScalarGridSpec(
            num_scalar_prefetch=1,
            grid=(5,),
            in_specs=[
                pl.BlockSpec(
                    (1, 2, boxes, rank, columns), lambda i, me: (jnp.minimum(i + 3, levels - 1), 0, 0, 0, 0)
                ),
                pl.BlockSpec((2, boxes, rank, columns), lambda i, me: (0, 0, 0, 0)),
            ],
            out_specs=[half_spec] * 4 + [third_spec] * 2,
        ),
        compiler_params=pltpu.CompilerParams(vmem_limit_bytes=ALL_VMEM_BYTES),
        cost_estimate=pl.CostEstimate(flops=0, bytes_accessed=5_000_000, transcendentals=0),
        name="late_blocks",
    )(me, weights, interp)


def order_kernel(in_ref, out_ref):
    for z_lo in range(2):
        for low in range(8):
            first = z_lo * 64 + low
            tile = jnp.concatenate(
                [in_ref[pl.ds(first, 4, stride=16)], in_ref[pl.ds(first + 8, 4, stride=16)]], 0
            )
            tile = jnp.swapaxes(tile, 0, 1)
            for box in range(8):
                row = ((box & 1) * 4 + (box >> 1)) * 128 + z_lo * 64 + low * 8
                out_ref[0, 0, row : row + 8] = tile[box]


def in_order(samples):
    senders, rows, columns = samples.shape
    return pl.pallas_call(
        order_kernel,
        out_shape=jax.ShapeDtypeStruct((2, rows // 16, senders * 8, columns), jnp.float32),
        grid=(rows // 8,),
        in_specs=[pl.BlockSpec((senders, 8, columns), lambda i: (0, i, 0))],
        out_specs=pl.BlockSpec((1, 1, senders * 8, columns), lambda i: (i % 2, i // 2, 0, 0)),
        compiler_params=pltpu.CompilerParams(vmem_limit_bytes=VMEM_BYTES),
        cost_estimate=pl.CostEstimate(flops=0, bytes_accessed=8_000_000, transcendentals=0),
        name="in_order",
    )(samples)


def on_device(source, weights, interp):
    groups_yz = [[g * 16 + (i & 1) * 8 + (i >> 1) * 2 + c for i in range(8)] for g in range(8) for c in range(2)]
    groups_y = [[g * 16 + z * 8 + y * 2 + c for y in range(4)] for g in range(8) for z in range(2) for c in range(2)]
    groups_xz = [[((i & 1) * 4 + (i >> 1)) * 16 + h for i in range(8)] for h in range(16)]
    gx, gy = lax.axis_index("gx"), lax.axis_index("gy")
    z_lo, x, z_hi = gx >> 2, gx & 3, gy >> 3

    def swap(value, groups):
        return lax.all_to_all(value, AXES, 0, 0, axis_index_groups=groups, tiled=True)

    bit = (gy & 1).astype(jnp.int32).reshape(1)
    me = jnp.stack([x, z_hi]).astype(jnp.int32)
    other = lax.ppermute(source, "gy", [(i, i ^ 1) for i in range(16)])
    early = swap(early_blocks(weights), groups_y)

    def z_move(value, mask):
        return lax.ppermute(value, AXES, [(i, i ^ mask) for i in range(128)])

    *pieces, keep3, give3 = late_blocks(me, weights, interp)
    other, pieces = lax.optimization_barrier((other, pieces))
    came3 = z_move(give3, 8)
    at_end = z_hi == z_lo
    cames = [z_move(give, 72) for give in pieces[2:]]
    state = first_level(bit, source, other, weights)
    state, early, cames[0] = lax.optimization_barrier((state, early, cames[0]))
    stay, turned = [], []
    for keep, came in zip(pieces[:2], cames):
        stay.append(jnp.where(at_end, keep, came))
        turned.append(z_move(jnp.where(at_end, came, keep), 64))
    state = swap(state, groups_y)
    state = y_levels(state, early)
    state, came3, stay, turned = lax.optimization_barrier((state, came3, stay, turned))
    state = swap(state, groups_yz)
    late = []
    for i in range(4):
        piece = jnp.stack([stay[i // 2][i % 2], turned[i // 2][i % 2]])
        late.append(lax.ppermute(piece, "gx", [(g, g ^ i) for g in range(8)]) if i else piece)
    state = z_level(me, state, keep3, came3)
    state, *late = lax.optimization_barrier((state, *late))
    state = swap(state, groups_xz)
    samples = last_levels(me, state, late)
    samples = samples.reshape(128, -1, samples.shape[-1])
    samples = lax.all_to_all(samples, AXES, 0, 0, tiled=True)
    return in_order(samples)


def solution(mesh):
    return jax.shard_map(
        on_device,
        mesh=mesh,
        in_specs=(
            P(None, ("gx", "gy"), None, None),
            P(None, None, ("gx", "gy"), None, None),
            P(None, ("gx", "gy"), None, None),
        ),
        out_specs=P(None, ("gx", "gy"), None, None),
        check_vma=False,
    )
```

```python
import jax
import jax.numpy as jnp
from jax import lax
from jax.experimental import pallas as pl
from jax.experimental.pallas import tpu as pltpu
from jax.sharding import PartitionSpec as P

AXES = ("gx", "gy")
TILE = 256
VMEM_BYTES = 48 * 1024 * 1024
ALL_VMEM_BYTES = 60 * 1024 * 1024


def halves(value):
    high = value.astype(jnp.bfloat16)
    return high, (value - high.astype(jnp.float32)).astype(jnp.bfloat16)


def dot3(a_high, a_low, b_high, b_low):
    left = jnp.concatenate([a_high, a_high, a_low], 1)
    right = jnp.concatenate([b_high, b_low, b_high], 0)
    return jnp.dot(left, right, preferred_element_type=jnp.float32)


def real_rows(real, imag):
    return jnp.concatenate([jnp.concatenate([real, -imag], 1), jnp.concatenate([imag, real], 1)], 0)


def first_level_kernel(bit_ref, own_ref, other_ref, w_ref, out_ref):
    swap = bit_ref[0] == 1
    for box in range(out_ref.shape[0]):
        real, imag = w_ref[0, 0, box], w_ref[0, 1, box]
        real = jnp.where(swap, pltpu.roll(real, 64, 1), real)
        imag = jnp.where(swap, pltpu.roll(imag, 64, 1), imag)
        block = real_rows(real, imag)
        coeffs = jnp.concatenate([own_ref[0, box], other_ref[0, box], own_ref[1, box], other_ref[1, box]], 0)
        out_ref[box] = dot3(*halves(block), *halves(coeffs))


def first_level(bit, own, other, weights):
    _, boxes, rank, frames = own.shape
    at_once = 2
    state = pl.BlockSpec((2, at_once, rank, frames), lambda k, bit: (0, k, 0, 0))
    return pl.pallas_call(
        first_level_kernel,
        out_shape=jax.ShapeDtypeStruct((boxes, 2 * rank, frames), jnp.float32),
        grid_spec=pltpu.PrefetchScalarGridSpec(
            num_scalar_prefetch=1,
            grid=(boxes // at_once,),
            in_specs=[
                state,
                state,
                pl.BlockSpec((1, 2, at_once, rank, 2 * rank), lambda k, bit: (0, 0, k, 0, 0)),
            ],
            out_specs=pl.BlockSpec((at_once, 2 * rank, frames), lambda k, bit: (k, 0, 0)),
        ),
        compiler_params=pltpu.CompilerParams(vmem_limit_bytes=VMEM_BYTES),
        cost_estimate=pl.CostEstimate(flops=900_000_000, bytes_accessed=7_000_000, transcendentals=0),
        name="first_level",
    )(bit, own, other, weights)


def one_level(state_ref, w_ref, at, pairs):
    rank = state_ref.shape[1] // 2
    for (low, w_low), (high, w_high) in pairs:
        block = jnp.concatenate(
            [real_rows(w_ref[w_low, at, 0], w_ref[w_low, at, 1]), real_rows(w_ref[w_high, at, 0], w_ref[w_high, at, 1])], 0
        )
        coeffs = jnp.concatenate(
            [state_ref[low, :rank], state_ref[high, :rank], state_ref[low, rank:], state_ref[high, rank:]], 0
        )
        new = dot3(*halves(block), *halves(coeffs))
        state_ref[low] = new[: 2 * rank]
        state_ref[high] = new[2 * rank :]


def pairs_of(mask):
    return [((b, b), (b | mask, b | mask)) for b in range(8) if not b & mask]


def y_levels_kernel(in_ref, w_ref, out_ref):
    out_ref[...] = in_ref[...]
    for at, mask in enumerate((2, 4)):
        one_level(out_ref, w_ref, at, pairs_of(mask))


def y_levels(state, weights):
    boxes, rows, frames = state.shape
    tile = pl.BlockSpec((boxes, rows, TILE), lambda i: (0, 0, i))
    return pl.pallas_call(
        y_levels_kernel,
        out_shape=pltpu.HBM(state.shape, jnp.float32),
        grid=(frames // TILE,),
        in_specs=[tile, pl.BlockSpec(weights.shape, lambda i: (0, 0, 0, 0, 0))],
        out_specs=tile,
        compiler_params=pltpu.CompilerParams(vmem_limit_bytes=VMEM_BYTES),
        cost_estimate=pl.CostEstimate(flops=1_800_000_000, bytes_accessed=5_000_000, transcendentals=0),
        name="y_levels",
    )(state, weights)


def z_level_kernel(mx_ref, mz_ref, in_ref, keep_ref, came_ref, out_ref, w_ref):
    w_ref[mz_ref[0], 0] = keep_ref[0]
    w_ref[1 - mz_ref[0], 0] = came_ref[0]
    out_ref[...] = in_ref[...]
    one_level(out_ref, w_ref, 0, [((0, 0), (1, 1))])


def z_level(me, state, keep, came):
    boxes, rows, frames = state.shape
    pair = pl.BlockSpec((2, rows, frames), lambda i, mx, mz: (i, 0, 0))
    block = pl.BlockSpec((1,) + keep.shape[1:], lambda i, mx, mz: (i, 0, 0, 0))
    return pl.pallas_call(
        z_level_kernel,
        out_shape=jax.ShapeDtypeStruct(state.shape, jnp.float32),
        grid_spec=pltpu.PrefetchScalarGridSpec(
            num_scalar_prefetch=2,
            grid=(boxes // 2,),
            in_specs=[pair, block, block],
            out_specs=pair,
            scratch_shapes=[pltpu.VMEM((2, 1) + keep.shape[1:], jnp.float32)],
        ),
        compiler_params=pltpu.CompilerParams(vmem_limit_bytes=VMEM_BYTES),
        cost_estimate=pl.CostEstimate(flops=900_000_000, bytes_accessed=4_500_000, transcendentals=0),
        name="z_level",
    )(*me, state, keep, came)


def last_levels_kernel(mx_ref, mz_ref, in_ref, *refs):
    *late_refs, out_ref, w_ref, state_ref = refs

    @pl.when(pl.program_id(0) == 0)
    def _():
        for i, late_ref in enumerate(late_refs):
            for j in range(2):
                w_ref[(mx_ref[0] ^ i) * 2 + (mz_ref[0] ^ j)] = late_ref[j]

    state_ref[...] = in_ref[...]
    for at, mask in enumerate((2, 4, 1)):
        one_level(state_ref, w_ref, at, pairs_of(mask))
    boxes = state_ref.shape[0]
    for box in range(boxes):
        real, imag = w_ref[box, 3, 0], w_ref[box, 3, 1]
        block = jnp.concatenate([jnp.concatenate([real, imag], 1), jnp.concatenate([-imag, real], 1)], 0)
        samples = dot3(*halves(jnp.transpose(state_ref[box])), *halves(block))
        columns = real.shape[1]
        count = samples.shape[0]
        out_ref[pl.ds(box, count, stride=2 * boxes), :] = samples[:, :columns]
        out_ref[pl.ds(boxes + box, count, stride=2 * boxes), :] = samples[:, columns:]


def last_levels(me, state, late):
    boxes, rows, frames = state.shape
    return pl.pallas_call(
        last_levels_kernel,
        out_shape=jax.ShapeDtypeStruct((frames * 2 * boxes, rows), jnp.float32),
        grid_spec=pltpu.PrefetchScalarGridSpec(
            num_scalar_prefetch=2,
            grid=(frames // TILE,),
            in_specs=[pl.BlockSpec((boxes, rows, TILE), lambda i, mx, mz: (0, 0, i))]
            + [pl.BlockSpec(late[0].shape, lambda i, mx, mz: (0, 0, 0, 0, 0))] * 4,
            out_specs=pl.BlockSpec((TILE * 2 * boxes, rows), lambda i, mx, mz: (i, 0)),
            scratch_shapes=[
                pltpu.VMEM((boxes,) + late[0].shape[1:], jnp.float32),
                pltpu.VMEM((boxes, rows, TILE), jnp.float32),
            ],
        ),
        compiler_params=pltpu.CompilerParams(vmem_limit_bytes=VMEM_BYTES),
        cost_estimate=pl.CostEstimate(flops=3_600_000_000, bytes_accessed=8_000_000, transcendentals=0),
        name="last_levels",
    )(*me, state, *late)


def pick(block_ref, part, box):
    return block_ref[(0,) * (len(block_ref.shape) - 4) + (part, box)]


def send_kernel(mx_ref, mz_ref, w1_ref, w2_ref, w4_ref, w5_ref, w6_ref, interp_ref, early_ref, *give_refs):
    for part in range(2):
        for at, block_ref in enumerate((w4_ref, w5_ref, w6_ref, interp_ref)):
            for i in range(4):
                give_refs[i // 2][i % 2, at, part] = pick(block_ref, part, (mx_ref[0] ^ i) * 2 + 1 - mz_ref[0])
        early_ref[:, 0, part] = w1_ref[0, part]
        early_ref[:, 1, part] = w2_ref[0, part]


def keep_kernel(mx_ref, mz_ref, w3_ref, w4_ref, w5_ref, w6_ref, interp_ref, keep1_ref, keep2_ref, keep3_ref, give3_ref):
    for part in range(2):
        for at, block_ref in enumerate((w4_ref, w5_ref, w6_ref, interp_ref)):
            for i in range(4):
                (keep1_ref, keep2_ref)[i // 2][i % 2, at, part] = pick(block_ref, part, (mx_ref[0] ^ i) * 2 + mz_ref[0])
        for high in range(4):
            keep3_ref[high, part] = pick(w3_ref, part, high * 2 + mz_ref[0])
            give3_ref[high, part] = pick(w3_ref, part, high * 2 + 1 - mz_ref[0])


def gather_call(kernel, name, levels, out_shapes, me, weights, interp):
    _, _, boxes, rank, columns = weights.shape

    def whole(shape):
        return pl.BlockSpec(shape, lambda i, mx, mz: (0,) * len(shape))

    def of_level(level):
        return pl.BlockSpec((1, 2, boxes, rank, columns), lambda i, mx, mz: (level, 0, 0, 0, 0))

    shapes = [shape + (2, rank, columns) for shape in out_shapes]
    return pl.pallas_call(
        kernel,
        out_shape=[jax.ShapeDtypeStruct(shape, jnp.float32) for shape in shapes],
        grid_spec=pltpu.PrefetchScalarGridSpec(
            num_scalar_prefetch=2,
            grid=(1,),
            in_specs=[of_level(level) for level in levels] + [whole(interp.shape)],
            out_specs=[whole(shape) for shape in shapes],
        ),
        compiler_params=pltpu.CompilerParams(vmem_limit_bytes=ALL_VMEM_BYTES),
        cost_estimate=pl.CostEstimate(flops=0, bytes_accessed=5_000_000, transcendentals=0),
        name=name,
    )(*me, *[weights] * len(levels), interp)


def order_kernel(in_ref, out_ref):
    for z_lo in range(2):
        for low in range(8):
            tile = jnp.swapaxes(in_ref[pl.ds(z_lo * 64 + low, 8, stride=8)], 0, 1)
            for box in range(8):
                row = ((box & 1) * 4 + (box >> 1)) * 128 + z_lo * 64 + low * 8
                out_ref[0, 0, row : row + 8] = tile[box]


def in_order(samples):
    senders, rows, columns = samples.shape
    return pl.pallas_call(
        order_kernel,
        out_shape=jax.ShapeDtypeStruct((2, rows // 16, senders * 8, columns), jnp.float32),
        grid=(rows // 8,),
        in_specs=[pl.BlockSpec((senders, 8, columns), lambda i: (0, i, 0))],
        out_specs=pl.BlockSpec((1, 1, senders * 8, columns), lambda i: (i % 2, i // 2, 0, 0)),
        compiler_params=pltpu.CompilerParams(vmem_limit_bytes=VMEM_BYTES),
        cost_estimate=pl.CostEstimate(flops=0, bytes_accessed=8_000_000, transcendentals=0),
        name="in_order",
    )(samples)


def on_device(source, weights, interp):
    groups_yz = [[g * 16 + (i & 1) * 8 + (i >> 1) * 2 + c for i in range(8)] for g in range(8) for c in range(2)]
    groups_y = [[g * 16 + z * 8 + y * 2 + c for y in range(4)] for g in range(8) for z in range(2) for c in range(2)]
    groups_xz = [[((i & 1) * 4 + (i >> 1)) * 16 + h for i in range(8)] for h in range(16)]
    gx, gy = lax.axis_index("gx"), lax.axis_index("gy")
    z_lo, x, z_hi = gx >> 2, gx & 3, gy >> 3

    def swap(value, groups):
        return lax.all_to_all(value, AXES, 0, 0, axis_index_groups=groups, tiled=True)

    bit = (gy & 1).astype(jnp.int32).reshape(1)
    me = [value.astype(jnp.int32).reshape(1) for value in (x, z_hi)]

    def z_move(value, mask):
        return lax.ppermute(value, AXES, [(i, i ^ mask) for i in range(128)])

    other = lax.ppermute(source, "gy", [(i, i ^ 1) for i in range(16)])
    early, *gives = gather_call(
        send_kernel, "send_blocks", (1, 2, 4, 5, 6), [(8, 2), (2, 4), (2, 4)], me, weights, interp
    )
    at_end = z_hi == z_lo
    cames = [z_move(give, 72) for give in gives]
    early = swap(early, groups_y)
    *keeps, keep3, give3 = gather_call(
        keep_kernel, "keep_blocks", (3, 4, 5, 6), [(2, 4), (2, 4), (4,), (4,)], me, weights, interp
    )
    other, keeps, keep3, give3 = lax.optimization_barrier((other, keeps, keep3, give3))
    came3 = z_move(give3, 8)
    state = first_level(bit, source, other, weights)
    state, early, cames[0] = lax.optimization_barrier((state, early, cames[0]))
    state = swap(state, groups_y)
    stay = [jnp.where(at_end, keep, came) for keep, came in zip(keeps, cames)]
    turned = [z_move(jnp.where(at_end, came, keep), 64) for keep, came in zip(keeps, cames)]
    state = y_levels(state, early)
    state, stay, turned = lax.optimization_barrier((state, stay, turned))
    state = swap(state, groups_yz)
    late = []
    for i in range(4):
        piece = jnp.stack([stay[i // 2][i % 2], turned[i // 2][i % 2]])
        late.append(lax.ppermute(piece, "gx", [(g, g ^ i) for g in range(8)]) if i else piece)
    state = z_level(me, state, keep3, came3)
    state, *late = lax.optimization_barrier((state, *late))
    state = swap(state, groups_xz)
    samples = last_levels(me, state, late)
    samples = samples.reshape(128, -1, samples.shape[-1])
    samples = lax.all_to_all(samples, AXES, 0, 0, tiled=True)
    return in_order(samples)


def solution(mesh):
    return jax.shard_map(
        on_device,
        mesh=mesh,
        in_specs=(
            P(None, ("gx", "gy"), None, None),
            P(None, None, ("gx", "gy"), None, None),
            P(None, ("gx", "gy"), None, None),
        ),
        out_specs=P(None, ("gx", "gy"), None, None),
        check_vma=False,
    )
```

```python
import jax
import jax.numpy as jnp
from jax import lax
from jax.experimental import pallas as pl
from jax.experimental.pallas import tpu as pltpu
from jax.sharding import PartitionSpec as P

AXES = ("gx", "gy")
TILE = 256
VMEM_BYTES = 48 * 1024 * 1024
ALL_VMEM_BYTES = 60 * 1024 * 1024


def halves(value):
    high = value.astype(jnp.bfloat16)
    return high, (value - high.astype(jnp.float32)).astype(jnp.bfloat16)


def dot3(a_high, a_low, b_high, b_low):
    left = jnp.concatenate([a_high, a_high, a_low], 1)
    right = jnp.concatenate([b_high, b_low, b_high], 0)
    return jnp.dot(left, right, preferred_element_type=jnp.float32)


def real_rows(real, imag):
    return jnp.concatenate([jnp.concatenate([real, -imag], 1), jnp.concatenate([imag, real], 1)], 0)


def first_level_kernel(bit_ref, own_ref, other_ref, w_ref, out_ref):
    swap = bit_ref[0] == 1
    for box in range(out_ref.shape[0]):
        real, imag = w_ref[0, 0, box], w_ref[0, 1, box]
        real = jnp.where(swap, pltpu.roll(real, 64, 1), real)
        imag = jnp.where(swap, pltpu.roll(imag, 64, 1), imag)
        block = real_rows(real, imag)
        coeffs = jnp.concatenate([own_ref[0, box], other_ref[0, box], own_ref[1, box], other_ref[1, box]], 0)
        out_ref[box] = dot3(*halves(block), *halves(coeffs))


def first_level(bit, own, other, weights):
    _, boxes, rank, frames = own.shape
    at_once = 2
    state = pl.BlockSpec((2, at_once, rank, frames), lambda k, bit: (0, k, 0, 0))
    return pl.pallas_call(
        first_level_kernel,
        out_shape=jax.ShapeDtypeStruct((boxes, 2 * rank, frames), jnp.float32),
        grid_spec=pltpu.PrefetchScalarGridSpec(
            num_scalar_prefetch=1,
            grid=(boxes // at_once,),
            in_specs=[
                state,
                state,
                pl.BlockSpec((1, 2, at_once, rank, 2 * rank), lambda k, bit: (0, 0, k, 0, 0)),
            ],
            out_specs=pl.BlockSpec((at_once, 2 * rank, frames), lambda k, bit: (k, 0, 0)),
        ),
        compiler_params=pltpu.CompilerParams(vmem_limit_bytes=VMEM_BYTES),
        cost_estimate=pl.CostEstimate(flops=900_000_000, bytes_accessed=7_000_000, transcendentals=0),
        name="first_level",
    )(bit, own, other, weights)


def one_level(state_ref, w_ref, at, pairs):
    rank = state_ref.shape[1] // 2
    for (low, w_low), (high, w_high) in pairs:
        block = jnp.concatenate(
            [real_rows(w_ref[w_low, at, 0], w_ref[w_low, at, 1]), real_rows(w_ref[w_high, at, 0], w_ref[w_high, at, 1])], 0
        )
        coeffs = jnp.concatenate(
            [state_ref[low, :rank], state_ref[high, :rank], state_ref[low, rank:], state_ref[high, rank:]], 0
        )
        new = dot3(*halves(block), *halves(coeffs))
        state_ref[low] = new[: 2 * rank]
        state_ref[high] = new[2 * rank :]


def pairs_of(mask):
    return [((b, b), (b | mask, b | mask)) for b in range(8) if not b & mask]


def y_levels_kernel(in_ref, w_ref, out_ref):
    out_ref[...] = in_ref[...]
    for at, mask in enumerate((2, 4)):
        one_level(out_ref, w_ref, at, pairs_of(mask))


def y_levels(state, weights):
    boxes, rows, frames = state.shape
    tile = pl.BlockSpec((boxes, rows, TILE), lambda i: (0, 0, i))
    return pl.pallas_call(
        y_levels_kernel,
        out_shape=pltpu.HBM(state.shape, jnp.float32),
        grid=(frames // TILE,),
        in_specs=[tile, pl.BlockSpec(weights.shape, lambda i: (0, 0, 0, 0, 0))],
        out_specs=tile,
        compiler_params=pltpu.CompilerParams(vmem_limit_bytes=VMEM_BYTES),
        cost_estimate=pl.CostEstimate(flops=1_800_000_000, bytes_accessed=5_000_000, transcendentals=0),
        name="y_levels",
    )(state, weights)


def z_level_kernel(mx_ref, mz_ref, in_ref, keep_ref, came_ref, out_ref, w_ref):
    w_ref[mz_ref[0], 0] = keep_ref[0]
    w_ref[1 - mz_ref[0], 0] = came_ref[0]
    out_ref[...] = in_ref[...]
    one_level(out_ref, w_ref, 0, [((0, 0), (1, 1))])


def z_level(me, state, keep, came):
    boxes, rows, frames = state.shape
    pair = pl.BlockSpec((2, rows, frames), lambda i, mx, mz: (i, 0, 0))
    block = pl.BlockSpec((1,) + keep.shape[1:], lambda i, mx, mz: (i, 0, 0, 0))
    return pl.pallas_call(
        z_level_kernel,
        out_shape=jax.ShapeDtypeStruct(state.shape, jnp.float32),
        grid_spec=pltpu.PrefetchScalarGridSpec(
            num_scalar_prefetch=2,
            grid=(boxes // 2,),
            in_specs=[pair, block, block],
            out_specs=pair,
            scratch_shapes=[pltpu.VMEM((2, 1) + keep.shape[1:], jnp.float32)],
        ),
        compiler_params=pltpu.CompilerParams(vmem_limit_bytes=VMEM_BYTES),
        cost_estimate=pl.CostEstimate(flops=900_000_000, bytes_accessed=4_500_000, transcendentals=0),
        name="z_level",
    )(*me, state, keep, came)


def last_levels_kernel(mx_ref, mz_ref, in_ref, *refs):
    *late_refs, out_ref, w_ref, state_ref = refs

    @pl.when(pl.program_id(0) == 0)
    def _():
        for i, late_ref in enumerate(late_refs):
            for j in range(2):
                w_ref[(mx_ref[0] ^ i) * 2 + (mz_ref[0] ^ j)] = late_ref[j]

    state_ref[...] = in_ref[...]
    for at, mask in enumerate((2, 4, 1)):
        one_level(state_ref, w_ref, at, pairs_of(mask))
    boxes = state_ref.shape[0]
    for box in range(boxes):
        real, imag = w_ref[box, 3, 0], w_ref[box, 3, 1]
        block = jnp.concatenate([jnp.concatenate([real, imag], 1), jnp.concatenate([-imag, real], 1)], 0)
        samples = dot3(*halves(jnp.transpose(state_ref[box])), *halves(block))
        columns = real.shape[1]
        count = samples.shape[0]
        out_ref[pl.ds(box, count, stride=2 * boxes), :] = samples[:, :columns]
        out_ref[pl.ds(boxes + box, count, stride=2 * boxes), :] = samples[:, columns:]


def last_levels(me, state, late):
    boxes, rows, frames = state.shape
    return pl.pallas_call(
        last_levels_kernel,
        out_shape=jax.ShapeDtypeStruct((frames * 2 * boxes, rows), jnp.float32),
        grid_spec=pltpu.PrefetchScalarGridSpec(
            num_scalar_prefetch=2,
            grid=(frames // TILE,),
            in_specs=[pl.BlockSpec((boxes, rows, TILE), lambda i, mx, mz: (0, 0, i))]
            + [pl.BlockSpec(late[0].shape, lambda i, mx, mz: (0, 0, 0, 0, 0))] * 4,
            out_specs=pl.BlockSpec((TILE * 2 * boxes, rows), lambda i, mx, mz: (i, 0)),
            scratch_shapes=[
                pltpu.VMEM((boxes,) + late[0].shape[1:], jnp.float32),
                pltpu.VMEM((boxes, rows, TILE), jnp.float32),
            ],
        ),
        compiler_params=pltpu.CompilerParams(vmem_limit_bytes=VMEM_BYTES),
        cost_estimate=pl.CostEstimate(flops=3_600_000_000, bytes_accessed=8_000_000, transcendentals=0),
        name="last_levels",
    )(*me, state, *late)


def pick(block_ref, part, box):
    return block_ref[(0,) * (len(block_ref.shape) - 4) + (part, box)]


def send_kernel(mx_ref, mz_ref, w1_ref, w2_ref, w4_ref, w5_ref, w6_ref, interp_ref, early_ref, *give_refs):
    for part in range(2):
        for at, block_ref in enumerate((w4_ref, w5_ref, w6_ref, interp_ref)):
            for i in range(4):
                give_refs[i // 2][i % 2, at, part] = pick(block_ref, part, (mx_ref[0] ^ i) * 2 + 1 - mz_ref[0])
        early_ref[:, 0, part] = w1_ref[0, part]
        early_ref[:, 1, part] = w2_ref[0, part]


def keep_kernel(mx_ref, mz_ref, w3_ref, w4_ref, w5_ref, w6_ref, interp_ref, keep1_ref, keep2_ref, keep3_ref, give3_ref):
    for part in range(2):
        for at, block_ref in enumerate((w4_ref, w5_ref, w6_ref, interp_ref)):
            for i in range(4):
                (keep1_ref, keep2_ref)[i // 2][i % 2, at, part] = pick(block_ref, part, (mx_ref[0] ^ i) * 2 + mz_ref[0])
        for high in range(4):
            keep3_ref[high, part] = pick(w3_ref, part, high * 2 + mz_ref[0])
            give3_ref[high, part] = pick(w3_ref, part, high * 2 + 1 - mz_ref[0])


def gather_call(kernel, name, levels, out_shapes, me, weights, interp):
    _, _, boxes, rank, columns = weights.shape

    def whole(shape):
        return pl.BlockSpec(shape, lambda i, mx, mz: (0,) * len(shape))

    def of_level(level):
        return pl.BlockSpec((1, 2, boxes, rank, columns), lambda i, mx, mz: (level, 0, 0, 0, 0))

    shapes = [shape + (2, rank, columns) for shape in out_shapes]
    return pl.pallas_call(
        kernel,
        out_shape=[jax.ShapeDtypeStruct(shape, jnp.float32) for shape in shapes],
        grid_spec=pltpu.PrefetchScalarGridSpec(
            num_scalar_prefetch=2,
            grid=(1,),
            in_specs=[of_level(level) for level in levels] + [whole(interp.shape)],
            out_specs=[whole(shape) for shape in shapes],
        ),
        compiler_params=pltpu.CompilerParams(vmem_limit_bytes=ALL_VMEM_BYTES),
        cost_estimate=pl.CostEstimate(flops=0, bytes_accessed=5_000_000, transcendentals=0),
        name=name,
    )(*me, *[weights] * len(levels), interp)


def order_kernel(in_ref, out_ref):
    for at in range(in_ref.shape[1] // 8):
        for z_lo in range(2):
            for low in range(8):
                tile = in_ref[pl.ds(z_lo * 64 + low, 8, stride=8), at * 8 : at * 8 + 8]
                tile = jnp.swapaxes(tile, 0, 1)
                for box in range(8):
                    row = ((box & 1) * 4 + (box >> 1)) * 128 + z_lo * 64 + low * 8
                    out_ref[at % 2, at // 2, row : row + 8] = tile[box]


def in_order(samples):
    senders, rows, columns = samples.shape
    return pl.pallas_call(
        order_kernel,
        out_shape=jax.ShapeDtypeStruct((2, rows // 16, senders * 8, columns), jnp.float32),
        grid=(rows // 32,),
        in_specs=[pl.BlockSpec((senders, 32, columns), lambda i: (0, i, 0))],
        out_specs=pl.BlockSpec((2, 2, senders * 8, columns), lambda i: (0, i, 0, 0)),
        compiler_params=pltpu.CompilerParams(vmem_limit_bytes=VMEM_BYTES),
        cost_estimate=pl.CostEstimate(flops=0, bytes_accessed=8_000_000, transcendentals=0),
        name="in_order",
    )(samples)


def on_device(source, weights, interp):
    groups_yz = [[g * 16 + (i & 1) * 8 + (i >> 1) * 2 + c for i in range(8)] for g in range(8) for c in range(2)]
    groups_y = [[g * 16 + z * 8 + y * 2 + c for y in range(4)] for g in range(8) for z in range(2) for c in range(2)]
    groups_xz = [[((i & 1) * 4 + (i >> 1)) * 16 + h for i in range(8)] for h in range(16)]
    gx, gy = lax.axis_index("gx"), lax.axis_index("gy")
    z_lo, x, z_hi = gx >> 2, gx & 3, gy >> 3

    def swap(value, groups):
        return lax.all_to_all(value, AXES, 0, 0, axis_index_groups=groups, tiled=True)

    bit = (gy & 1).astype(jnp.int32).reshape(1)
    me = [value.astype(jnp.int32).reshape(1) for value in (x, z_hi)]

    def z_move(value, mask):
        return lax.ppermute(value, AXES, [(i, i ^ mask) for i in range(128)])

    other = lax.ppermute(source, "gy", [(i, i ^ 1) for i in range(16)])
    early, *gives = gather_call(
        send_kernel, "send_blocks", (1, 2, 4, 5, 6), [(8, 2), (2, 4), (2, 4)], me, weights, interp
    )
    at_end = z_hi == z_lo
    cames = [z_move(give, 72) for give in gives]
    early = swap(early, groups_y)
    *keeps, keep3, give3 = gather_call(
        keep_kernel, "keep_blocks", (3, 4, 5, 6), [(2, 4), (2, 4), (4,), (4,)], me, weights, interp
    )
    other, keeps, keep3, give3 = lax.optimization_barrier((other, keeps, keep3, give3))
    came3 = z_move(give3, 8)
    state = first_level(bit, source, other, weights)
    state, early, cames[0] = lax.optimization_barrier((state, early, cames[0]))
    state = swap(state, groups_y)
    stay = [jnp.where(at_end, keep, came) for keep, came in zip(keeps, cames)]
    turned = [z_move(jnp.where(at_end, came, keep), 64) for keep, came in zip(keeps, cames)]
    state = y_levels(state, early)
    state, stay, turned = lax.optimization_barrier((state, stay, turned))
    state = swap(state, groups_yz)
    late = []
    for i in range(4):
        piece = jnp.stack([stay[i // 2][i % 2], turned[i // 2][i % 2]])
        late.append(lax.ppermute(piece, "gx", [(g, g ^ i) for g in range(8)]) if i else piece)
    state = z_level(me, state, keep3, came3)
    state, *late = lax.optimization_barrier((state, *late))
    state = swap(state, groups_xz)
    samples = last_levels(me, state, late)
    samples = samples.reshape(128, -1, samples.shape[-1])
    samples = lax.all_to_all(samples, AXES, 0, 0, tiled=True)
    return in_order(samples)


def solution(mesh):
    return jax.shard_map(
        on_device,
        mesh=mesh,
        in_specs=(
            P(None, ("gx", "gy"), None, None),
            P(None, None, ("gx", "gy"), None, None),
            P(None, ("gx", "gy"), None, None),
        ),
        out_specs=P(None, ("gx", "gy"), None, None),
        check_vma=False,
    )
```

```python
import jax
import jax.numpy as jnp
from jax import lax
from jax.experimental import pallas as pl
from jax.experimental.pallas import tpu as pltpu
from jax.sharding import PartitionSpec as P

AXES = ("gx", "gy")
TILE = 256
VMEM_BYTES = 48 * 1024 * 1024
ALL_VMEM_BYTES = 60 * 1024 * 1024


def halves(value):
    high = value.astype(jnp.bfloat16)
    return high, (value - high.astype(jnp.float32)).astype(jnp.bfloat16)


def dot3(a_high, a_low, b_high, b_low):
    left = jnp.concatenate([a_high, a_high, a_low], 1)
    right = jnp.concatenate([b_high, b_low, b_high], 0)
    return jnp.dot(left, right, preferred_element_type=jnp.float32)


def real_rows(real, imag):
    return jnp.concatenate([jnp.concatenate([real, -imag], 1), jnp.concatenate([imag, real], 1)], 0)


def first_level_kernel(bit_ref, own_ref, other_ref, w_ref, out_ref):
    swap = bit_ref[0] == 1
    for box in range(out_ref.shape[0]):
        real, imag = w_ref[0, 0, box], w_ref[0, 1, box]
        real = jnp.where(swap, pltpu.roll(real, 64, 1), real)
        imag = jnp.where(swap, pltpu.roll(imag, 64, 1), imag)
        block = real_rows(real, imag)
        coeffs = jnp.concatenate([own_ref[0, box], other_ref[0, box], own_ref[1, box], other_ref[1, box]], 0)
        out_ref[box] = dot3(*halves(block), *halves(coeffs))


def first_level(bit, own, other, weights):
    _, boxes, rank, frames = own.shape
    at_once = 2
    state = pl.BlockSpec((2, at_once, rank, frames), lambda k, bit: (0, k, 0, 0))
    return pl.pallas_call(
        first_level_kernel,
        out_shape=jax.ShapeDtypeStruct((boxes, 2 * rank, frames), jnp.float32),
        grid_spec=pltpu.PrefetchScalarGridSpec(
            num_scalar_prefetch=1,
            grid=(boxes // at_once,),
            in_specs=[
                state,
                state,
                pl.BlockSpec((1, 2, at_once, rank, 2 * rank), lambda k, bit: (0, 0, k, 0, 0)),
            ],
            out_specs=pl.BlockSpec((at_once, 2 * rank, frames), lambda k, bit: (k, 0, 0)),
        ),
        compiler_params=pltpu.CompilerParams(vmem_limit_bytes=VMEM_BYTES),
        cost_estimate=pl.CostEstimate(flops=900_000_000, bytes_accessed=7_000_000, transcendentals=0),
        name="first_level",
    )(bit, own, other, weights)


def one_level(state_ref, w_ref, at, pairs):
    rank = state_ref.shape[1] // 2
    for (low, w_low), (high, w_high) in pairs:
        block = jnp.concatenate(
            [real_rows(w_ref[w_low, at, 0], w_ref[w_low, at, 1]), real_rows(w_ref[w_high, at, 0], w_ref[w_high, at, 1])], 0
        )
        coeffs = jnp.concatenate(
            [state_ref[low, :rank], state_ref[high, :rank], state_ref[low, rank:], state_ref[high, rank:]], 0
        )
        new = dot3(*halves(block), *halves(coeffs))
        state_ref[low] = new[: 2 * rank]
        state_ref[high] = new[2 * rank :]


def pairs_of(mask):
    return [((b, b), (b | mask, b | mask)) for b in range(8) if not b & mask]


def y_levels_kernel(in_ref, w_ref, out_ref):
    out_ref[...] = in_ref[...]
    for at, mask in enumerate((2, 4)):
        one_level(out_ref, w_ref, at, pairs_of(mask))


def y_levels(state, weights):
    boxes, rows, frames = state.shape
    tile = pl.BlockSpec((boxes, rows, frames), lambda i: (0, 0, i))
    return pl.pallas_call(
        y_levels_kernel,
        out_shape=pltpu.HBM(state.shape, jnp.float32),
        grid=(frames // frames,),
        in_specs=[tile, pl.BlockSpec(weights.shape, lambda i: (0, 0, 0, 0, 0))],
        out_specs=tile,
        compiler_params=pltpu.CompilerParams(vmem_limit_bytes=VMEM_BYTES),
        cost_estimate=pl.CostEstimate(flops=1_800_000_000, bytes_accessed=5_000_000, transcendentals=0),
        name="y_levels",
    )(state, weights)


def z_level_kernel(mx_ref, mz_ref, in_ref, keep_ref, came_ref, out_ref, w_ref):
    count = keep_ref.shape[0]
    for high in range(count):
        w_ref[high * 2 + mz_ref[0], 0] = keep_ref[high]
        w_ref[high * 2 + 1 - mz_ref[0], 0] = came_ref[high]
    out_ref[...] = in_ref[...]
    one_level(out_ref, w_ref, 0, [((b, b), (b + 1, b + 1)) for b in range(0, 2 * count, 2)])


def z_level(me, state, keep, came):
    boxes, rows, frames = state.shape
    pair = pl.BlockSpec((4, rows, frames), lambda i, mx, mz: (i, 0, 0))
    block = pl.BlockSpec((2,) + keep.shape[1:], lambda i, mx, mz: (i, 0, 0, 0))
    return pl.pallas_call(
        z_level_kernel,
        out_shape=jax.ShapeDtypeStruct(state.shape, jnp.float32),
        grid_spec=pltpu.PrefetchScalarGridSpec(
            num_scalar_prefetch=2,
            grid=(boxes // 4,),
            in_specs=[pair, block, block],
            out_specs=pair,
            scratch_shapes=[pltpu.VMEM((4, 1) + keep.shape[1:], jnp.float32)],
        ),
        compiler_params=pltpu.CompilerParams(vmem_limit_bytes=VMEM_BYTES),
        cost_estimate=pl.CostEstimate(flops=900_000_000, bytes_accessed=4_500_000, transcendentals=0),
        name="z_level",
    )(*me, state, keep, came)


def last_levels_kernel(mx_ref, mz_ref, in_ref, *refs):
    *late_refs, out_ref, w_ref, state_ref = refs

    @pl.when(pl.program_id(0) == 0)
    def _():
        for i, late_ref in enumerate(late_refs):
            for j in range(2):
                w_ref[(mx_ref[0] ^ i) * 2 + (mz_ref[0] ^ j)] = late_ref[j]

    state_ref[...] = in_ref[...]
    for at, mask in enumerate((2, 4, 1)):
        one_level(state_ref, w_ref, at, pairs_of(mask))
    boxes = state_ref.shape[0]
    for box in range(boxes):
        real, imag = w_ref[box, 3, 0], w_ref[box, 3, 1]
        block = jnp.concatenate([jnp.concatenate([real, imag], 1), jnp.concatenate([-imag, real], 1)], 0)
        samples = dot3(*halves(jnp.transpose(state_ref[box])), *halves(block))
        columns = real.shape[1]
        count = samples.shape[0]
        out_ref[pl.ds(box, count, stride=2 * boxes), :] = samples[:, :columns]
        out_ref[pl.ds(boxes + box, count, stride=2 * boxes), :] = samples[:, columns:]


def last_levels(me, state, late):
    boxes, rows, frames = state.shape
    return pl.pallas_call(
        last_levels_kernel,
        out_shape=jax.ShapeDtypeStruct((frames * 2 * boxes, rows), jnp.float32),
        grid_spec=pltpu.PrefetchScalarGridSpec(
            num_scalar_prefetch=2,
            grid=(frames // TILE,),
            in_specs=[pl.BlockSpec((boxes, rows, TILE), lambda i, mx, mz: (0, 0, i))]
            + [pl.BlockSpec(late[0].shape, lambda i, mx, mz: (0, 0, 0, 0, 0))] * 4,
            out_specs=pl.BlockSpec((TILE * 2 * boxes, rows), lambda i, mx, mz: (i, 0)),
            scratch_shapes=[
                pltpu.VMEM((boxes,) + late[0].shape[1:], jnp.float32),
                pltpu.VMEM((boxes, rows, TILE), jnp.float32),
            ],
        ),
        compiler_params=pltpu.CompilerParams(vmem_limit_bytes=VMEM_BYTES),
        cost_estimate=pl.CostEstimate(flops=3_600_000_000, bytes_accessed=8_000_000, transcendentals=0),
        name="last_levels",
    )(*me, state, *late)


def pick(block_ref, part, box):
    return block_ref[(0,) * (len(block_ref.shape) - 4) + (part, box)]


def send_kernel(mx_ref, mz_ref, w1_ref, w2_ref, w4_ref, w5_ref, w6_ref, interp_ref, early_ref, *give_refs):
    for part in range(2):
        for at, block_ref in enumerate((w4_ref, w5_ref, w6_ref, interp_ref)):
            for i in range(4):
                give_refs[i // 2][i % 2, at, part] = pick(block_ref, part, (mx_ref[0] ^ i) * 2 + 1 - mz_ref[0])
        early_ref[:, 0, part] = w1_ref[0, part]
        early_ref[:, 1, part] = w2_ref[0, part]


def keep_kernel(mx_ref, mz_ref, w3_ref, w4_ref, w5_ref, w6_ref, interp_ref, keep1_ref, keep2_ref, keep3_ref, give3_ref):
    for part in range(2):
        for at, block_ref in enumerate((w4_ref, w5_ref, w6_ref, interp_ref)):
            for i in range(4):
                (keep1_ref, keep2_ref)[i // 2][i % 2, at, part] = pick(block_ref, part, (mx_ref[0] ^ i) * 2 + mz_ref[0])
        for high in range(4):
            keep3_ref[high, part] = pick(w3_ref, part, high * 2 + mz_ref[0])
            give3_ref[high, part] = pick(w3_ref, part, high * 2 + 1 - mz_ref[0])


def gather_call(kernel, name, levels, out_shapes, me, weights, interp):
    _, _, boxes, rank, columns = weights.shape

    def whole(shape):
        return pl.BlockSpec(shape, lambda i, mx, mz: (0,) * len(shape))

    def of_level(level):
        return pl.BlockSpec((1, 2, boxes, rank, columns), lambda i, mx, mz: (level, 0, 0, 0, 0))

    shapes = [shape + (2, rank, columns) for shape in out_shapes]
    return pl.pallas_call(
        kernel,
        out_shape=[jax.ShapeDtypeStruct(shape, jnp.float32) for shape in shapes],
        grid_spec=pltpu.PrefetchScalarGridSpec(
            num_scalar_prefetch=2,
            grid=(1,),
            in_specs=[of_level(level) for level in levels] + [whole(interp.shape)],
            out_specs=[whole(shape) for shape in shapes],
        ),
        compiler_params=pltpu.CompilerParams(vmem_limit_bytes=ALL_VMEM_BYTES),
        cost_estimate=pl.CostEstimate(flops=0, bytes_accessed=5_000_000, transcendentals=0),
        name=name,
    )(*me, *[weights] * len(levels), interp)


def order_kernel(in_ref, out_ref):
    for at in range(in_ref.shape[1] // 8):
        for z_lo in range(2):
            for low in range(8):
                tile = in_ref[pl.ds(z_lo * 64 + low, 8, stride=8), at * 8 : at * 8 + 8]
                tile = jnp.swapaxes(tile, 0, 1)
                for box in range(8):
                    row = ((box & 1) * 4 + (box >> 1)) * 128 + z_lo * 64 + low * 8
                    out_ref[at % 2, at // 2, row : row + 8] = tile[box]


def in_order(samples):
    senders, rows, columns = samples.shape
    return pl.pallas_call(
        order_kernel,
        out_shape=jax.ShapeDtypeStruct((2, rows // 16, senders * 8, columns), jnp.float32),
        grid=(rows // 32,),
        in_specs=[pl.BlockSpec((senders, 32, columns), lambda i: (0, i, 0))],
        out_specs=pl.BlockSpec((2, 2, senders * 8, columns), lambda i: (0, i, 0, 0)),
        compiler_params=pltpu.CompilerParams(vmem_limit_bytes=VMEM_BYTES),
        cost_estimate=pl.CostEstimate(flops=0, bytes_accessed=8_000_000, transcendentals=0),
        name="in_order",
    )(samples)


def on_device(source, weights, interp):
    groups_yz = [[g * 16 + (i & 1) * 8 + (i >> 1) * 2 + c for i in range(8)] for g in range(8) for c in range(2)]
    groups_y = [[g * 16 + z * 8 + y * 2 + c for y in range(4)] for g in range(8) for z in range(2) for c in range(2)]
    groups_xz = [[((i & 1) * 4 + (i >> 1)) * 16 + h for i in range(8)] for h in range(16)]
    gx, gy = lax.axis_index("gx"), lax.axis_index("gy")
    z_lo, x, z_hi = gx >> 2, gx & 3, gy >> 3

    def swap(value, groups):
        return lax.all_to_all(value, AXES, 0, 0, axis_index_groups=groups, tiled=True)

    bit = (gy & 1).astype(jnp.int32).reshape(1)
    me = [value.astype(jnp.int32).reshape(1) for value in (x, z_hi)]

    def z_move(value, mask):
        return lax.ppermute(value, AXES, [(i, i ^ mask) for i in range(128)])

    other = lax.ppermute(source, "gy", [(i, i ^ 1) for i in range(16)])
    early, *gives = gather_call(
        send_kernel, "send_blocks", (1, 2, 4, 5, 6), [(8, 2), (2, 4), (2, 4)], me, weights, interp
    )
    at_end = z_hi == z_lo
    cames = [z_move(give, 72) for give in gives]
    early = swap(early, groups_y)
    *keeps, keep3, give3 = gather_call(
        keep_kernel, "keep_blocks", (3, 4, 5, 6), [(2, 4), (2, 4), (4,), (4,)], me, weights, interp
    )
    other, keeps, keep3, give3 = lax.optimization_barrier((other, keeps, keep3, give3))
    came3 = z_move(give3, 8)
    state = first_level(bit, source, other, weights)
    state, early, cames[0] = lax.optimization_barrier((state, early, cames[0]))
    state = swap(state, groups_y)
    stay = [jnp.where(at_end, keep, came) for keep, came in zip(keeps, cames)]
    turned = [z_move(jnp.where(at_end, came, keep), 64) for keep, came in zip(keeps, cames)]
    state = y_levels(state, early)
    state, stay, turned = lax.optimization_barrier((state, stay, turned))
    state = swap(state, groups_yz)
    late = []
    for i in range(4):
        piece = jnp.stack([stay[i // 2][i % 2], turned[i // 2][i % 2]])
        late.append(lax.ppermute(piece, "gx", [(g, g ^ i) for g in range(8)]) if i else piece)
    state = z_level(me, state, keep3, came3)
    state, *late = lax.optimization_barrier((state, *late))
    state = swap(state, groups_xz)
    samples = last_levels(me, state, late)
    samples = samples.reshape(128, -1, samples.shape[-1])
    samples = lax.all_to_all(samples, AXES, 0, 0, tiled=True)
    return in_order(samples)


def solution(mesh):
    return jax.shard_map(
        on_device,
        mesh=mesh,
        in_specs=(
            P(None, ("gx", "gy"), None, None),
            P(None, None, ("gx", "gy"), None, None),
            P(None, ("gx", "gy"), None, None),
        ),
        out_specs=P(None, ("gx", "gy"), None, None),
        check_vma=False,
    )
```
